32 devices in a mesh: rows: 8 (over z, x), rep: 4 (over y, core).
Axes of the slice: x: 2, y: 2, z: 4, core: 2. Of those that a mesh axis runs over, the one named last changes fastest.
Arguments:
- features: bfloat16 [4096, 256], P(('rows', 'rep')), may hold values from -6 to 6
- weight: bfloat16 [256, 256], replicated, may hold values from -0.375 to 0.375
- bias_terms: float32 [256], replicated, may hold values from -3 to 3
- tile_data: bfloat16 [8, 4, 8, 128, 128], P('rows'), may hold values from -0.1875 to 0.1875
- tile_row: int32 [8, 4, 8], P('rows'), may hold values from 0 to 3
- tile_col: int32 [8, 4, 8], P('rows'), may hold values from 0 to 7
- tile_count: int32 [8, 4], P('rows'), may hold values from 1 to 8, as said below
- grad_out: bfloat16 [4096, 256], P(('rows', 'rep')), may hold values from -6 to 6
Outputs:
- layer_out: bfloat16 [4096, 256], P(('rows', 'rep'))
- weight_grad: float32 [256, 256], replicated
- bias_grad: float32 [256], replicated
The draws below stay inside these ranges and needn't reach their ends.
Inputs may be any that keep to these rules, and one draw needn't show every extreme that they name: `tile_count`: some group's stripe has all 8 slots live in every draw.
All inputs are finite; a program needn't handle non-finite values.
Results may differ from the reference program's by a relative error of at most 0.015.
Values may be sent and summed in bfloat16 or wider, within the bound.
A program may use at most 64 MiB of HBM per device.

```python
import jax
import jax.numpy as jnp
from jax import lax

F = 256
BLOCK = 128
CAP = 8
NBLK = 32
NODES = 4096
N_ROWS = 8
N_REP = 4


def draw_tile_count(key, part):
    first_key, second_key, third_key = jax.random.split(key, 3)
    base_counts = jax.random.randint(first_key, (N_ROWS, N_REP), 1, CAP // 2 + 1)
    full_flags = jax.random.randint(second_key, (N_ROWS, N_REP), 0, 8) == 0
    counts = jnp.where(full_flags, CAP, base_counts)
    spot = jax.random.randint(third_key, (), 0, N_ROWS * N_REP)
    flat_counts = counts.reshape(-1).at[spot].set(CAP)
    return flat_counts.reshape(N_ROWS, N_REP).astype(jnp.int32)


def plant(result, key, least, top_value):
    extent = result.shape
    index_at = [jax.random.randint(jax.random.fold_in(key, axis), (), 0, extent[axis]) for axis in range(len(extent))]
    result = result.at[tuple(index_at)].set(least)
    longest = extent.index(max(extent))
    index_at[longest] = (index_at[longest] + 1) % extent[longest]
    return result.at[tuple(index_at)].set(top_value)


def level_of(rng, extent, shards, least, top_value):
    gain, own = 1.0, jax.random.fold_in(rng, 6)
    for position, shards_of in shards:
        heights = jnp.exp(jax.random.uniform(jax.random.fold_in(own, position), (shards_of,), jnp.float32, least / len(shards), top_value / len(shards)))
        gain = gain * jnp.repeat(heights, extent[position] // shards_of).reshape([-1 if axis == position else 1 for axis in range(len(extent))])
    return gain


def normal_values(rng, shape, scale, reach, cuts=(), kind=jnp.bfloat16):
    drawn = scale * jax.random.normal(rng, shape, jnp.float32)
    if cuts:
        drawn = drawn * level_of(rng, shape, cuts, -0.22, 0.18)
    return jnp.clip(drawn, -reach, reach).astype(kind)


def setup_inputs(seed: int = 0) -> dict:
    arg_keys = jax.random.split(jax.random.key(seed), 9)
    return {
        "features": normal_values(arg_keys[0], (NODES, F), 1.0, 6.0, ((0, 32),)),
        "weight": normal_values(arg_keys[1], (F, F), F ** -0.5, 0.375),
        "bias_terms": normal_values(arg_keys[2], (F,), 0.5, 3.0, (), jnp.float32),
        "tile_data": normal_values(arg_keys[3], (N_ROWS, N_REP, CAP, BLOCK, BLOCK), (BLOCK * CAP) ** -0.5, 0.1875, ((0, 8),)),
        "tile_row": plant(jax.random.randint(arg_keys[4], (N_ROWS, N_REP, CAP), 0, N_REP), jax.random.fold_in(arg_keys[4], 1), 0, N_REP - 1).astype(jnp.int32),
        "tile_col": plant(jax.random.randint(arg_keys[5], (N_ROWS, N_REP, CAP), 0, N_ROWS), jax.random.fold_in(arg_keys[5], 1), 0, N_ROWS - 1).astype(jnp.int32),
        "tile_count": draw_tile_count(jax.random.fold_in(arg_keys[8], 71), 0),
        "grad_out": normal_values(arg_keys[7], (NODES, F), 1.0, 6.0, ((0, 32),)),
    }


def reference(features, weight, bias_terms, tile_data, tile_row, tile_col, tile_count, grad_out):
    blocks_all = features.reshape(NBLK, BLOCK, F)
    stripe_ids = jnp.arange(N_REP, dtype=jnp.int32)
    slot_ids = jnp.arange(CAP, dtype=jnp.int32)

    def one_group(packed):
        tile_grp, row_grp, col_grp, count_grp = packed
        global_col = (col_grp * N_REP + stripe_ids[:, None]).astype(jnp.int32)
        picked = blocks_all[global_col.reshape(-1)].astype(jnp.float32)
        product = jnp.einsum("tij,tjf->tif", tile_grp.reshape(-1, BLOCK, BLOCK).astype(jnp.float32), picked)
        live = (slot_ids[None, :] < count_grp[:, None]).reshape(-1)
        select = ((row_grp.reshape(-1)[None, :] == stripe_ids[:, None]) & live[None, :]).astype(jnp.float32)
        return jnp.einsum("bt,tif->bif", select, product)

    summed = lax.map(one_group, (tile_data, tile_row, tile_col, tile_count))
    propagated = summed.reshape(NODES, F).astype(jnp.bfloat16)
    preact = jnp.dot(propagated, weight, preferred_element_type=jnp.float32) + bias_terms
    sig = jax.nn.sigmoid(preact)
    layer_out = (preact * sig).astype(jnp.bfloat16)
    slope = sig * (1.0 + preact * (1.0 - sig))
    grad_pre = (grad_out.astype(jnp.float32) * slope).astype(jnp.bfloat16)
    weight_grad = jnp.dot(propagated.T, grad_pre, preferred_element_type=jnp.float32)
    bias_grad = jnp.sum(grad_pre.astype(jnp.float32), axis=0)
    return layer_out, weight_grad, bias_grad
```

```python
import functools

import jax
import jax.numpy as jnp
from jax import lax
from jax.experimental import pallas as pl
from jax.experimental.pallas import tpu as pltpu
from jax.sharding import PartitionSpec as P

MESH = pl.DeviceIdType.MESH


def xor(value, mask):
    bit = 1
    while bit <= mask:
        if mask & bit:
            value = value + bit - 2 * bit * ((value // bit) % 2)
        bit *= 2
    return value


def kernel(
    n_rows, n_rep, staged,
    feat_hbm, weight_hbm, bias_hbm, tile_hbm, row_ref, col_ref, count_ref, gout_hbm,
    out_ref, wgrad_ref, bgrad_ref,
    feat, tiles, weight, bias, gout, part, part_in, term, term_in, slab, piece, piece_in,
    local_sem, g_send, g_recv, x_send, x_recv, w1_send, w1_recv,
    w2_send, w2_recv, w3_send, w3_recv, w4_send, w4_recv,
):
    me = lax.axis_index("rows")
    rep = lax.axis_index("rep")
    capacity, block = tiles.shape[0], tiles.shape[1]
    width = weight.shape[1]
    own_rows = width // n_rep

    loads = [
        pltpu.make_async_copy(feat_hbm, feat.at[me], local_sem.at[0]),
        pltpu.make_async_copy(tile_hbm.at[0, rep], tiles, local_sem.at[1]),
        pltpu.make_async_copy(weight_hbm, weight, local_sem.at[2]),
        pltpu.make_async_copy(bias_hbm, bias, local_sem.at[3]),
        pltpu.make_async_copy(gout_hbm, gout, local_sem.at[4]),
    ]
    for load in loads:
        load.start()

    def to_rows(mask, src, dst, send, recv):
        return pltpu.make_async_remote_copy(
            src_ref=src, dst_ref=dst, send_sem=send, recv_sem=recv,
            device_id=(xor(me, mask), rep), device_id_type=MESH)

    def to_rep(mask, src, dst, send, recv):
        return pltpu.make_async_remote_copy(
            src_ref=src, dst_ref=dst, send_sem=send, recv_sem=recv,
            device_id=(me, xor(rep, mask)), device_id_type=MESH)

    barrier = pltpu.get_barrier_semaphore()
    for mask in range(1, n_rows):
        pl.semaphore_signal(barrier, inc=1, device_id=(xor(me, mask), rep), device_id_type=MESH)
    for mask in range(1, n_rep):
        pl.semaphore_signal(barrier, inc=1, device_id=(me, xor(rep, mask)), device_id_type=MESH)
    pl.semaphore_wait(barrier, n_rows + n_rep - 2)

    def gather(mask, block_mask, sem):
        where = feat.at[xor(me, block_mask)]
        source = feat_hbm if block_mask == 0 else where
        return to_rows(mask, source, where, g_send.at[sem], g_recv.at[sem])

    sends = [gather(1, 0, 1)]
    for mask in range(2, n_rows, 2):
        sends.append(gather(mask, 0, mask))
    for send in sends:
        send.start()

    def arrived(mask):
        where = feat.at[xor(me, mask)]
        to_rows(1, where, where, g_send.at[mask], g_recv.at[mask]).wait_recv()

    for mask in range(2, n_rows, 2):
        arrived(mask)
        send = gather(1, mask, mask + 1)
        send.start()
        sends.append(send)
    for mask in range(1, n_rows, 2):
        arrived(mask)
    loads[0].wait()
    loads[1].wait()

    rows_of = [row_ref[0, rep, slot] for slot in range(capacity)]
    live = [slot < count_ref[0, rep] for slot in range(capacity)]
    picked = jnp.concatenate([feat[col_ref[0, rep, slot]] for slot in range(capacity)], axis=0)
    none = jnp.zeros((block, block), jnp.bfloat16)

    def wide(target):
        return jnp.concatenate(
            [jnp.where((rows_of[slot] == target) & live[slot], tiles[slot], none)
             for slot in range(capacity)], axis=1)

    stacked = jnp.concatenate([wide(xor(rep, mask)) for mask in range(n_rep)], axis=0)
    partial = jnp.dot(stacked, picked, preferred_element_type=jnp.float32)
    part[...] = partial[block:].reshape(n_rep - 1, block, width).astype(jnp.bfloat16)
    exchange = [
        to_rep(mask, part.at[mask - 1], part_in.at[mask - 1], x_send.at[mask - 1], x_recv.at[mask - 1])
        for mask in range(1, n_rep)
    ]
    for copy in reversed(exchange):
        copy.start()
    for load in loads[2:]:
        load.wait()
    total = partial[:block]
    for mask in range(1, n_rep):
        exchange[mask - 1].wait_recv()
        total = total + part_in[mask - 1].astype(jnp.float32)

    propagated = total.astype(jnp.bfloat16)
    preact = jnp.dot(propagated, weight[...], preferred_element_type=jnp.float32) + bias[...]
    sigma = jax.nn.sigmoid(preact)
    slope = sigma * (1.0 + preact * (1.0 - sigma))
    grad_pre = (gout[...].astype(jnp.float32) * slope).astype(jnp.bfloat16)
    weight_term = lax.dot_general(
        propagated, grad_pre, (((0,), (0,)), ((), ())), preferred_element_type=jnp.float32)
    bias_term = jnp.sum(grad_pre.astype(jnp.float32).reshape(block // 8, 8, width), axis=0)
    for place in range(n_rep):
        term[place, :own_rows] = weight_term[place * own_rows:(place + 1) * own_rows]
        term[place, own_rows:] = bias_term

    scatter = [
        to_rep(mask, term.at[xor(rep, mask)], term_in.at[mask - 1], w1_send.at[mask - 1], w1_recv.at[mask - 1])
        for mask in range(1, n_rep)
    ]
    for copy in reversed(scatter):
        copy.start()
    out_ref[...] = (preact * sigma).astype(jnp.bfloat16)
    mine = term[rep]
    for mask in range(1, n_rep):
        scatter[mask - 1].wait_recv()
        mine = mine + term_in[mask - 1]

    base = pl.multiple_of(rep * own_rows, own_rows)
    pending = []
    if staged:
        share = own_rows // n_rows
        for place in range(n_rows):
            piece[place, :share] = mine[place * share:(place + 1) * share]
            piece[place, share:] = mine[own_rows:]
        spread = [
            to_rows(mask, piece.at[xor(me, mask)], piece_in.at[mask - 1],
                    w2_send.at[mask - 1], w2_recv.at[mask - 1])
            for mask in range(1, n_rows)
        ]
        for copy in spread:
            copy.start()
        done = piece[me]
        for mask in range(1, n_rows):
            spread[mask - 1].wait_recv()
            done = done + piece_in[mask - 1]
        final_bias = done[share:]

        def share_of(index):
            return wgrad_ref.at[pl.ds(pl.multiple_of(base + index * share, share), share)]

        wgrad_ref[pl.ds(pl.multiple_of(base + me * share, share), share)] = done[:share]
        back = [
            to_rows(mask, share_of(me), share_of(me), w3_send.at[mask - 1], w3_recv.at[mask - 1])
            for mask in range(1, n_rows)
        ]
        for copy in back:
            copy.start()
        for mask in range(1, n_rows):
            where = share_of(xor(me, mask))
            to_rows(mask, where, where, w3_send.at[mask - 1], w3_recv.at[mask - 1]).wait_recv()
        pending = spread + back
    else:
        step = 0
        while (1 << step) < n_rows:
            slab[step] = mine
            copy = to_rows(1 << step, slab.at[step], piece_in.at[step], w2_send.at[step], w2_recv.at[step])
            copy.start()
            copy.wait_recv()
            mine = mine + piece_in[step]
            pending.append(copy)
            step += 1
        final_bias = mine[own_rows:]
        wgrad_ref[pl.ds(base, own_rows)] = mine[:own_rows]

    def slab_of(index):
        return wgrad_ref.at[pl.ds(pl.multiple_of(index * own_rows, own_rows), own_rows)]

    final = [
        to_rep(mask, slab_of(rep), slab_of(rep), w4_send.at[mask - 1], w4_recv.at[mask - 1])
        for mask in range(1, n_rep)
    ]
    for copy in reversed(final):
        copy.start()
    bgrad_ref[...] = jnp.sum(final_bias, axis=0, keepdims=True)
    for copy in sends + exchange + scatter + pending + final:
        copy.wait_send()
    for mask in range(1, n_rep):
        where = slab_of(xor(rep, mask))
        to_rep(mask, where, where, w4_send.at[mask - 1], w4_recv.at[mask - 1]).wait_recv()


def shards(features, weight, bias_terms, tile_data, tile_row, tile_col, tile_count, grad_out):
    n_rows, n_rep = lax.axis_size("rows"), lax.axis_size("rep")
    block, width = features.shape
    capacity = tile_data.shape[2]
    own_rows = width // n_rep
    staged = own_rows % (8 * n_rows) == 0
    share = own_rows // n_rows if staged else 8
    steps = 1 if staged else (n_rows - 1).bit_length()
    whole = (own_rows + 8, width)
    vmem = pl.BlockSpec(memory_space=pltpu.VMEM)
    smem = pl.BlockSpec(memory_space=pltpu.SMEM)
    hbm = pl.BlockSpec(memory_space=pl.ANY)
    dma = pltpu.SemaphoreType.DMA
    layer_out, weight_grad, bias_grad = pl.pallas_call(
        functools.partial(kernel, n_rows, n_rep, staged),
        out_shape=(
            jax.ShapeDtypeStruct((block, width), jnp.bfloat16),
            jax.ShapeDtypeStruct((width, width), jnp.float32),
            jax.ShapeDtypeStruct((1, width), jnp.float32),
        ),
        in_specs=[hbm, hbm, hbm, hbm, smem, smem, smem, hbm],
        out_specs=(vmem, vmem, vmem),
        scratch_shapes=[
            pltpu.VMEM((n_rows, block, width), jnp.bfloat16),
            pltpu.VMEM((capacity, block, block), jnp.bfloat16),
            pltpu.VMEM((width, width), jnp.bfloat16),
            pltpu.VMEM((1, width), jnp.float32),
            pltpu.VMEM((block, width), jnp.bfloat16),
            pltpu.VMEM((n_rep - 1, block, width), jnp.bfloat16),
            pltpu.VMEM((n_rep - 1, block, width), jnp.bfloat16),
            pltpu.VMEM((n_rep,) + whole, jnp.float32),
            pltpu.VMEM((n_rep - 1,) + whole, jnp.float32),
            pltpu.VMEM((steps,) + whole, jnp.float32),
            pltpu.VMEM((n_rows, share + 8, width), jnp.float32),
            pltpu.VMEM((n_rows - 1, share + 8, width) if staged else (steps,) + whole, jnp.float32),
            dma((5,)),
            dma((n_rows,)), dma((n_rows,)),
            dma((n_rep - 1,)), dma((n_rep - 1,)),
            dma((n_rep - 1,)), dma((n_rep - 1,)),
            dma((n_rows - 1,)), dma((n_rows - 1,)),
            dma((n_rows - 1,)), dma((n_rows - 1,)),
            dma((n_rep - 1,)), dma((n_rep - 1,)),
        ],
        compiler_params=pltpu.CompilerParams(
            collective_id=0, has_side_effects=True, vmem_limit_bytes=40 * 1024 * 1024),
    )(features, weight, bias_terms.reshape(1, width), tile_data, tile_row, tile_col, tile_count, grad_out)
    return layer_out, weight_grad, bias_grad.reshape(width)


def solution(mesh):
    placed = (
        P(("rows", "rep"), None),
        P(),
        P(),
        P("rows", None, None, None, None),
        P("rows", None, None),
        P("rows", None, None),
        P("rows", None),
        P(("rows", "rep"), None),
    )
    return jax.shard_map(
        shards,
        mesh=mesh,
        in_specs=placed,
        out_specs=(P(("rows", "rep"), None), P(), P()),
        check_vma=False,
    )
```

```python
import functools

import jax
import jax.numpy as jnp
from jax import lax
from jax.experimental import pallas as pl
from jax.experimental.pallas import tpu as pltpu
from jax.sharding import PartitionSpec as P

MESH = pl.DeviceIdType.MESH
SHARE_TYPE = jnp.bfloat16


def xor(value, mask):
    bit = 1
    while bit <= mask:
        if mask & bit:
            value = value + bit - 2 * bit * ((value // bit) % 2)
        bit *= 2
    return value


def kernel(
    n_rows, n_rep, direct,
    feat_hbm, weight_hbm, bias_hbm, tile_hbm, row_hbm, col_hbm, count_hbm, gout_hbm,
    out_ref, wgrad_ref, bgrad_ref,
    feat, tiles, weight, bias, gout, part, part_in, term, term_in, ring, ring_in, bias_out, bias_in, piece, piece_in, share_in,
    row_ref, col_ref, count_ref, local_sem, g_send, g_recv, x_send, x_recv, w1_send, w1_recv,
    w2_send, w2_recv, w4_send, w4_recv, d_sem, b_sem,
):
    me = lax.axis_index("rows")
    rep = lax.axis_index("rep")
    capacity, block = tiles.shape[0], tiles.shape[1]
    width = weight.shape[1]
    own_rows = width // n_rep

    def to_rows(mask, src, dst, send, recv):
        return pltpu.make_async_remote_copy(
            src_ref=src, dst_ref=dst, send_sem=send, recv_sem=recv,
            device_id=(xor(me, mask), rep), device_id_type=MESH)

    def to_rep(mask, src, dst, send, recv):
        return pltpu.make_async_remote_copy(
            src_ref=src, dst_ref=dst, send_sem=send, recv_sem=recv,
            device_id=(me, xor(rep, mask)), device_id_type=MESH)

    barrier = pltpu.get_barrier_semaphore()
    for mask in range(1, n_rows):
        pl.semaphore_signal(barrier, inc=1, device_id=(xor(me, mask), rep), device_id_type=MESH)
    for mask in range(1, n_rep):
        pl.semaphore_signal(barrier, inc=1, device_id=(me, xor(rep, mask)), device_id_type=MESH)
    loads = [
        pltpu.make_async_copy(feat_hbm, feat.at[me], local_sem.at[0]),
        pltpu.make_async_copy(tile_hbm.at[0, rep], tiles, local_sem.at[1]),
        pltpu.make_async_copy(weight_hbm, weight, local_sem.at[2]),
        pltpu.make_async_copy(bias_hbm, bias, local_sem.at[3]),
        pltpu.make_async_copy(gout_hbm, gout, local_sem.at[4]),
        pltpu.make_async_copy(row_hbm, row_ref, local_sem.at[5]),
        pltpu.make_async_copy(col_hbm, col_ref, local_sem.at[6]),
        pltpu.make_async_copy(count_hbm, count_ref, local_sem.at[7]),
    ]
    for load in loads:
        load.start()
    pl.semaphore_wait(barrier, n_rows + n_rep - 2)

    def gather(mask, block_mask, sem):
        where = feat.at[xor(me, block_mask)]
        source = feat_hbm if block_mask == 0 else where
        return to_rows(mask, source, where, g_send.at[sem], g_recv.at[sem])

    sends = [gather(1, 0, 1)]
    for mask in range(2, n_rows, 2):
        sends.append(gather(mask, 0, mask))
    for send in sends:
        send.start()

    def arrived(mask):
        where = feat.at[xor(me, mask)]
        to_rows(1, where, where, g_send.at[mask], g_recv.at[mask]).wait_recv()

    for mask in range(2, n_rows, 2):
        arrived(mask)
        send = gather(1, mask, mask + 1)
        send.start()
        sends.append(send)
    for mask in range(1, n_rows, 2):
        arrived(mask)
    loads[0].wait()
    loads[1].wait()
    for load in loads[5:]:
        load.wait()

    rows_of = [row_ref[0, rep, slot] for slot in range(capacity)]
    live = [slot < count_ref[0, rep] for slot in range(capacity)]
    picked = jnp.concatenate([feat[col_ref[0, rep, slot]] for slot in range(capacity)], axis=0)
    none = jnp.zeros((block, block), jnp.bfloat16)

    def wide(target):
        return jnp.concatenate(
            [jnp.where((rows_of[slot] == target) & live[slot], tiles[slot], none)
             for slot in range(capacity)], axis=1)

    stacked = jnp.concatenate([wide(xor(rep, mask)) for mask in range(n_rep)], axis=0)
    partial = jnp.dot(stacked, picked, preferred_element_type=jnp.float32)
    part[...] = partial[block:].reshape(n_rep - 1, block, width).astype(jnp.bfloat16)
    exchange = [
        to_rep(mask, part.at[mask - 1], part_in.at[mask - 1], x_send.at[mask - 1], x_recv.at[mask - 1])
        for mask in range(1, n_rep)
    ]
    for copy in reversed(exchange):
        copy.start()
    for load in loads[2:5]:
        load.wait()
    total = partial[:block]
    for mask in range(1, n_rep):
        exchange[mask - 1].wait_recv()
        total = total + part_in[mask - 1].astype(jnp.float32)

    propagated = total.astype(jnp.bfloat16)
    preact = jnp.dot(propagated, weight[...], preferred_element_type=jnp.float32) + bias[...]
    sigma = jax.nn.sigmoid(preact)
    slope = sigma * (1.0 + preact * (1.0 - sigma))
    grad_pre = (gout[...].astype(jnp.float32) * slope).astype(jnp.bfloat16)
    weight_term = lax.dot_general(
        propagated, grad_pre, (((0,), (0,)), ((), ())), preferred_element_type=jnp.float32)
    bias_term = jnp.sum(grad_pre.astype(jnp.float32).reshape(block // 8, 8, width), axis=0)
    if direct:
        n_all = n_rows * n_rep
        here = me * n_rep + rep
        piece_rows, piece_cols = piece.shape[1:]
        across = width // piece_cols

        def place_of(index):
            top, left = index // across * piece_rows, index % across * piece_cols
            return slice(top, top + piece_rows), slice(left, left + piece_cols)

        def to_all(mask, src, dst, stage):
            peer = (xor(me, mask // n_rep), xor(rep, mask % n_rep))
            return pltpu.make_async_remote_copy(
                src_ref=src, dst_ref=dst, send_sem=d_sem.at[2 * stage], recv_sem=d_sem.at[2 * stage + 1],
                device_id=peer, device_id_type=MESH)

        order = sorted(range(1, n_all), key=lambda mask: -mask)
        for index in range(n_all):
            piece[index] = weight_term[place_of(index)].astype(jnp.bfloat16)
        for mask in order:
            to_all(mask, piece.at[xor(here, mask)], piece_in.at[mask - 1], 0).start()
        bias_out[0] = jnp.sum(bias_term, axis=0, keepdims=True)
        bias_rep = [
            to_rep(mask, bias_out.at[0], bias_in.at[mask - 1], b_sem.at[0, mask - 1], b_sem.at[1, mask - 1])
            for mask in range(1, n_rep)
        ]
        for copy in bias_rep:
            copy.start()
        out_ref[...] = (preact * sigma).astype(jnp.bfloat16)
        bias_sum = bias_out[0]
        for mask in range(1, n_rep):
            bias_rep[mask - 1].wait_recv()
            bias_sum = bias_sum + bias_in[mask - 1]
        bias_out[1] = bias_sum
        bias_rows = [
            to_rows(mask, bias_out.at[1], bias_in.at[n_rep - 2 + mask],
                    b_sem.at[0, n_rep - 2 + mask], b_sem.at[1, n_rep - 2 + mask])
            for mask in range(1, n_rows)
        ]
        done = piece[here].astype(jnp.float32)
        pltpu.make_async_copy(piece_in, piece_in, d_sem.at[1]).wait()
        for mask in range(1, n_all):
            done = done + piece_in[mask - 1].astype(jnp.float32)
        share_in[here] = done.astype(share_in.dtype)
        for mask in order:
            to_all(mask, share_in.at[here], share_in.at[here], 1).start()
        for copy in bias_rows:
            copy.start()
        for mask in range(1, n_rows):
            bias_rows[mask - 1].wait_recv()
            bias_sum = bias_sum + bias_in[n_rep - 2 + mask]
        bgrad_ref[...] = bias_sum
        for copy in sends + exchange + bias_rep + bias_rows:
            copy.wait_send()
        others = share_in.at[pl.ds(0, n_all - 1)]
        pltpu.make_async_copy(piece_in, piece_in, d_sem.at[0]).wait()
        pltpu.make_async_copy(others, others, d_sem.at[3]).wait()
        for index in range(n_all):
            wgrad_ref[place_of(index)] = share_in[index].astype(jnp.float32)
        pltpu.make_async_copy(others, others, d_sem.at[2]).wait()
        return

    for place in range(n_rep):
        term[place, :own_rows] = weight_term[place * own_rows:(place + 1) * own_rows]
        term[place, own_rows:] = bias_term
    scatter = [
        to_rep(mask, term.at[xor(rep, mask)], term_in.at[mask - 1], w1_send.at[mask - 1], w1_recv.at[mask - 1])
        for mask in range(1, n_rep)
    ]
    for copy in reversed(scatter):
        copy.start()
    out_ref[...] = (preact * sigma).astype(jnp.bfloat16)
    mine = term[rep]
    for mask in range(1, n_rep):
        scatter[mask - 1].wait_recv()
        mine = mine + term_in[mask - 1]
    base = pl.multiple_of(rep * own_rows, own_rows)
    pending = []
    step = 0
    while (1 << step) < n_rows:
        ring[step] = mine
        copy = to_rows(1 << step, ring.at[step], ring_in.at[step], w2_send.at[step], w2_recv.at[step])
        copy.start()
        copy.wait_recv()
        mine = mine + ring_in[step]
        pending.append(copy)
        step += 1
    wgrad_ref[pl.ds(base, own_rows)] = mine[:own_rows]

    def slab_of(index):
        return wgrad_ref.at[pl.ds(pl.multiple_of(index * own_rows, own_rows), own_rows)]

    final = [
        to_rep(mask, slab_of(rep), slab_of(rep), w4_send.at[mask - 1], w4_recv.at[mask - 1])
        for mask in range(1, n_rep)
    ]
    for copy in reversed(final):
        copy.start()
    bgrad_ref[...] = jnp.sum(mine[own_rows:], axis=0, keepdims=True)
    for copy in sends + exchange + scatter + pending + final:
        copy.wait_send()
    for mask in range(1, n_rep):
        where = slab_of(xor(rep, mask))
        to_rep(mask, where, where, w4_send.at[mask - 1], w4_recv.at[mask - 1]).wait_recv()


def shards(features, weight, bias_terms, tile_data, tile_row, tile_col, tile_count, grad_out):
    n_rows, n_rep = lax.axis_size("rows"), lax.axis_size("rep")
    block, width = features.shape
    capacity = tile_data.shape[2]
    own_rows = width // n_rep
    n_all = n_rows * n_rep
    direct = width * width == n_all * 16 * 128
    steps = 1 if direct else (n_rows - 1).bit_length()
    places = n_all if direct else 2
    whole = (own_rows + 8, width)
    vmem = pl.BlockSpec(memory_space=pltpu.VMEM)
    hbm = pl.BlockSpec(memory_space=pl.ANY)
    dma = pltpu.SemaphoreType.DMA
    layer_out, weight_grad, bias_grad = pl.pallas_call(
        functools.partial(kernel, n_rows, n_rep, direct),
        out_shape=(
            jax.ShapeDtypeStruct((block, width), jnp.bfloat16),
            jax.ShapeDtypeStruct((width, width), jnp.float32),
            jax.ShapeDtypeStruct((1, width), jnp.float32),
        ),
        in_specs=[hbm] * 8,
        out_specs=(vmem, vmem, vmem),
        scratch_shapes=[
            pltpu.VMEM((n_rows, block, width), jnp.bfloat16),
            pltpu.VMEM((capacity, block, block), jnp.bfloat16),
            pltpu.VMEM((width, width), jnp.bfloat16),
            pltpu.VMEM((1, width), jnp.float32),
            pltpu.VMEM((block, width), jnp.bfloat16),
            pltpu.VMEM((n_rep - 1, block, width), jnp.bfloat16),
            pltpu.VMEM((n_rep - 1, block, width), jnp.bfloat16),
            pltpu.VMEM((n_rep,) + whole, jnp.float32),
            pltpu.VMEM((n_rep - 1,) + whole, jnp.float32),
            pltpu.VMEM((steps,) + whole, jnp.float32),
            pltpu.VMEM((steps,) + whole, jnp.float32),
            pltpu.VMEM((2, 1, width), jnp.float32),
            pltpu.VMEM((n_rep + n_rows - 2, 1, width), jnp.float32),
            pltpu.VMEM((places, 16, 128), jnp.bfloat16),
            pltpu.VMEM((places - 1, 16, 128), jnp.bfloat16),
            pltpu.VMEM((places, 16, 128), SHARE_TYPE),
            pltpu.SMEM(tile_row.shape, jnp.int32),
            pltpu.SMEM(tile_col.shape, jnp.int32),
            pltpu.SMEM(tile_count.shape, jnp.int32),
            dma((8,)),
            dma((n_rows,)), dma((n_rows,)),
            dma((n_rep - 1,)), dma((n_rep - 1,)),
            dma((n_rep - 1,)), dma((n_rep - 1,)),
            dma((steps,)), dma((steps,)),
            dma((n_rep - 1,)), dma((n_rep - 1,)),
            dma((4,)),
            dma((2, n_rep + n_rows - 2)),
        ],
        compiler_params=pltpu.CompilerParams(
            collective_id=0, has_side_effects=True, vmem_limit_bytes=62 * 1024 * 1024),
    )(features, weight, bias_terms.reshape(1, width), tile_data, tile_row, tile_col, tile_count, grad_out)
    return layer_out, weight_grad, bias_grad.reshape(width)


def solution(mesh):
    placed = (
        P(("rows", "rep"), None),
        P(),
        P(),
        P("rows", None, None, None, None),
        P("rows", None, None),
        P("rows", None, None),
        P("rows", None),
        P(("rows", "rep"), None),
    )
    return jax.shard_map(
        shards,
        mesh=mesh,
        in_specs=placed,
        out_specs=(P(("rows", "rep"), None), P(), P()),
        check_vma=False,
    )
```

```python
import functools

import jax
import jax.numpy as jnp
from jax import lax
from jax.experimental import pallas as pl
from jax.experimental.pallas import tpu as pltpu
from jax.sharding import PartitionSpec as P

MESH = pl.DeviceIdType.MESH


def xor(value, mask):
    bit = 1
    while bit <= mask:
        if mask & bit:
            value = value + bit - 2 * bit * ((value // bit) % 2)
        bit *= 2
    return value


def kernel(
    n_rows, n_rep, direct,
    feat_hbm, weight_hbm, bias_hbm, tile_hbm, row_hbm, col_hbm, count_hbm, gout_hbm,
    out_ref, wgrad_ref, bgrad_ref,
    feat, tiles, weight, bias, gout, part, part_in, term, term_in, ring, ring_in, bias_out, bias_in,
    halves, half_in, piece, piece_in, share_in,
    row_ref, col_ref, count_ref, local_sem, g_send, g_recv, x_send, x_recv, w1_send, w1_recv,
    w2_send, w2_recv, w4_send, w4_recv, d_sem, b_sem,
):
    me = lax.axis_index("rows")
    rep = lax.axis_index("rep")
    capacity, block = tiles.shape[0], tiles.shape[1]
    width = weight.shape[1]
    own_rows = width // n_rep

    def to_rows(mask, src, dst, send, recv):
        return pltpu.make_async_remote_copy(
            src_ref=src, dst_ref=dst, send_sem=send, recv_sem=recv,
            device_id=(xor(me, mask), rep), device_id_type=MESH)

    def to_rep(mask, src, dst, send, recv):
        return pltpu.make_async_remote_copy(
            src_ref=src, dst_ref=dst, send_sem=send, recv_sem=recv,
            device_id=(me, xor(rep, mask)), device_id_type=MESH)

    barrier = pltpu.get_barrier_semaphore()
    for mask in range(1, n_rows):
        pl.semaphore_signal(barrier, inc=1, device_id=(xor(me, mask), rep), device_id_type=MESH)
    for mask in range(1, n_rep):
        pl.semaphore_signal(barrier, inc=1, device_id=(me, xor(rep, mask)), device_id_type=MESH)
    loads = [
        pltpu.make_async_copy(feat_hbm, feat.at[me], local_sem.at[0]),
        pltpu.make_async_copy(tile_hbm.at[0, rep], tiles, local_sem.at[1]),
        pltpu.make_async_copy(weight_hbm, weight, local_sem.at[2]),
        pltpu.make_async_copy(bias_hbm, bias, local_sem.at[3]),
        pltpu.make_async_copy(gout_hbm, gout, local_sem.at[4]),
        pltpu.make_async_copy(row_hbm, row_ref, local_sem.at[5]),
        pltpu.make_async_copy(col_hbm, col_ref, local_sem.at[6]),
        pltpu.make_async_copy(count_hbm, count_ref, local_sem.at[7]),
    ]
    for load in loads:
        load.start()
    loads[0].wait()
    pl.semaphore_wait(barrier, n_rows + n_rep - 2)

    def gather(mask, block_mask, sem):
        where = feat.at[xor(me, block_mask)]
        return to_rows(mask, where, where, g_send.at[sem], g_recv.at[sem])

    sends = [gather(1, 0, 1)]
    for mask in range(2, n_rows, 2):
        sends.append(gather(mask, 0, mask))
    for send in sends:
        send.start()

    def arrived(mask):
        where = feat.at[xor(me, mask)]
        to_rows(1, where, where, g_send.at[mask], g_recv.at[mask]).wait_recv()

    for mask in range(2, n_rows, 2):
        arrived(mask)
        send = gather(1, mask, mask + 1)
        send.start()
        sends.append(send)
    for mask in range(1, n_rows, 2):
        arrived(mask)
    loads[1].wait()
    for load in loads[5:]:
        load.wait()

    rows_of = [row_ref[0, rep, slot] for slot in range(capacity)]
    live = [slot < count_ref[0, rep] for slot in range(capacity)]
    picked = jnp.concatenate([feat[col_ref[0, rep, slot]] for slot in range(capacity)], axis=0)
    none = jnp.zeros((block, block), jnp.bfloat16)

    def wide(target):
        return jnp.concatenate(
            [jnp.where((rows_of[slot] == target) & live[slot], tiles[slot], none)
             for slot in range(capacity)], axis=1)

    stacked = jnp.concatenate([wide(xor(rep, mask)) for mask in range(n_rep)], axis=0)
    partial = jnp.dot(stacked, picked, preferred_element_type=jnp.float32)
    part[...] = partial[block:].reshape(n_rep - 1, block, width).astype(jnp.bfloat16)
    exchange = [
        to_rep(mask, part.at[mask - 1], part_in.at[mask - 1], x_send.at[mask - 1], x_recv.at[mask - 1])
        for mask in range(1, n_rep)
    ]
    for copy in reversed(exchange):
        copy.start()
    for load in loads[2:5]:
        load.wait()
    total = partial[:block]
    for mask in range(1, n_rep):
        exchange[mask - 1].wait_recv()
        total = total + part_in[mask - 1].astype(jnp.float32)

    propagated = total.astype(jnp.bfloat16)
    preact = jnp.dot(propagated, weight[...], preferred_element_type=jnp.float32) + bias[...]
    sigma = jax.nn.sigmoid(preact)
    slope = sigma * (1.0 + preact * (1.0 - sigma))
    grad_pre = (gout[...].astype(jnp.float32) * slope).astype(jnp.bfloat16)
    weight_term = lax.dot_general(
        propagated, grad_pre, (((0,), (0,)), ((), ())), preferred_element_type=jnp.float32)
    bias_term = jnp.sum(grad_pre.astype(jnp.float32).reshape(block // 8, 8, width), axis=0)
    if direct:
        n_pairs = n_rows * n_rep // 2
        pair, side = me * (n_rep // 2) + rep // 2, rep % 2
        piece_rows, piece_cols = piece.shape[1:]
        across = width // piece_cols

        def place_of(index):
            top, left = index // across * piece_rows, index % across * piece_cols
            return slice(top, top + piece_rows), slice(left, left + piece_cols)

        def to_pair(mask, src, dst, stage):
            peer = (xor(me, mask // (n_rep // 2)), xor(rep, mask % (n_rep // 2) * 2))
            return pltpu.make_async_remote_copy(
                src_ref=src, dst_ref=dst, send_sem=d_sem.at[2 * stage], recv_sem=d_sem.at[2 * stage + 1],
                device_id=peer, device_id_type=MESH)

        for index in range(2 * n_pairs):
            halves[index % 2, index // 2] = weight_term[place_of(index)]
        fold = to_rep(1, halves.at[xor(side, 1)], half_in, d_sem.at[4], d_sem.at[5])
        fold.start()
        bias_out[0] = jnp.sum(bias_term, axis=0, keepdims=True)
        bias_rep = [
            to_rep(mask, bias_out.at[0], bias_in.at[mask - 1], b_sem.at[0, mask - 1], b_sem.at[1, mask - 1])
            for mask in range(1, n_rep)
        ]
        for copy in bias_rep:
            copy.start()
        out_ref[...] = (preact * sigma).astype(jnp.bfloat16)
        order = list(range(n_pairs - 1, 0, -1))
        fold.wait_recv()
        piece[...] = (halves[side] + half_in[...]).astype(jnp.bfloat16)
        for mask in order:
            to_pair(mask, piece.at[xor(pair, mask)], piece_in.at[mask - 1], 0).start()
        bias_sum = bias_out[0]
        for mask in range(1, n_rep):
            bias_rep[mask - 1].wait_recv()
            bias_sum = bias_sum + bias_in[mask - 1]
        bias_out[1] = bias_sum
        bias_rows = [
            to_rows(mask, bias_out.at[1], bias_in.at[n_rep - 2 + mask],
                    b_sem.at[0, n_rep - 2 + mask], b_sem.at[1, n_rep - 2 + mask])
            for mask in range(1, n_rows)
        ]
        for copy in bias_rows:
            copy.start()
        done = piece[pair].astype(jnp.float32)
        pltpu.make_async_copy(piece_in, piece_in, d_sem.at[1]).wait()
        for mask in range(1, n_pairs):
            done = done + piece_in[mask - 1].astype(jnp.float32)
        share_in[side, pair] = done.astype(jnp.bfloat16)
        for mask in order:
            to_pair(mask, share_in.at[side, pair], share_in.at[side, pair], 1).start()
        for mask in range(1, n_rows):
            bias_rows[mask - 1].wait_recv()
            bias_sum = bias_sum + bias_in[n_rep - 2 + mask]
        bgrad_ref[...] = bias_sum
        for copy in sends + exchange + bias_rep + bias_rows + [fold]:
            copy.wait_send()
        pltpu.make_async_copy(piece_in, piece_in, d_sem.at[0]).wait()
        pltpu.make_async_copy(piece_in, piece_in, d_sem.at[3]).wait()
        hand = to_rep(1, share_in.at[side], share_in.at[side], d_sem.at[6], d_sem.at[7])
        hand.start()
        theirs = share_in.at[xor(side, 1)]
        to_rep(1, theirs, theirs, d_sem.at[6], d_sem.at[7]).wait_recv()
        for index in range(2 * n_pairs):
            wgrad_ref[place_of(index)] = share_in[index % 2, index // 2].astype(jnp.float32)
        hand.wait_send()
        pltpu.make_async_copy(piece_in, piece_in, d_sem.at[2]).wait()
        return

    for place in range(n_rep):
        term[place, :own_rows] = weight_term[place * own_rows:(place + 1) * own_rows]
        term[place, own_rows:] = bias_term
    scatter = [
        to_rep(mask, term.at[xor(rep, mask)], term_in.at[mask - 1], w1_send.at[mask - 1], w1_recv.at[mask - 1])
        for mask in range(1, n_rep)
    ]
    for copy in reversed(scatter):
        copy.start()
    out_ref[...] = (preact * sigma).astype(jnp.bfloat16)
    mine = term[rep]
    for mask in range(1, n_rep):
        scatter[mask - 1].wait_recv()
        mine = mine + term_in[mask - 1]
    base = pl.multiple_of(rep * own_rows, own_rows)
    pending = []
    step = 0
    while (1 << step) < n_rows:
        ring[step] = mine
        copy = to_rows(1 << step, ring.at[step], ring_in.at[step], w2_send.at[step], w2_recv.at[step])
        copy.start()
        copy.wait_recv()
        mine = mine + ring_in[step]
        pending.append(copy)
        step += 1
    wgrad_ref[pl.ds(base, own_rows)] = mine[:own_rows]

    def slab_of(index):
        return wgrad_ref.at[pl.ds(pl.multiple_of(index * own_rows, own_rows), own_rows)]

    final = [
        to_rep(mask, slab_of(rep), slab_of(rep), w4_send.at[mask - 1], w4_recv.at[mask - 1])
        for mask in range(1, n_rep)
    ]
    for copy in reversed(final):
        copy.start()
    bgrad_ref[...] = jnp.sum(mine[own_rows:], axis=0, keepdims=True)
    for copy in sends + exchange + scatter + pending + final:
        copy.wait_send()
    for mask in range(1, n_rep):
        where = slab_of(xor(rep, mask))
        to_rep(mask, where, where, w4_send.at[mask - 1], w4_recv.at[mask - 1]).wait_recv()


def deliver(first, second, third, first_out, second_out, third_out):
    first_out[...] = first[...]
    second_out[...] = second[...]
    third_out[...] = third[...]


def shards(features, weight, bias_terms, tile_data, tile_row, tile_col, tile_count, grad_out):
    n_rows, n_rep = lax.axis_size("rows"), lax.axis_size("rep")
    block, width = features.shape
    capacity = tile_data.shape[2]
    own_rows = width // n_rep
    n_all = n_rows * n_rep
    direct = width * width == n_all * 16 * 128
    steps = 1 if direct else (n_rows - 1).bit_length()
    pairs = n_all // 2 if direct else 2
    whole = (own_rows + 8, width)
    vmem = pl.BlockSpec(memory_space=pltpu.VMEM)
    hbm = pl.BlockSpec(memory_space=pl.ANY)
    dma = pltpu.SemaphoreType.DMA
    layer_out, weight_grad, bias_grad = pl.pallas_call(
        functools.partial(kernel, n_rows, n_rep, direct),
        out_shape=(
            jax.ShapeDtypeStruct((block, width), jnp.bfloat16),
            jax.ShapeDtypeStruct((width, width), jnp.float32),
            jax.ShapeDtypeStruct((1, width), jnp.float32),
        ),
        in_specs=[hbm] * 8,
        out_specs=(vmem, vmem, vmem),
        scratch_shapes=[
            pltpu.VMEM((n_rows, block, width), jnp.bfloat16),
            pltpu.VMEM((capacity, block, block), jnp.bfloat16),
            pltpu.VMEM((width, width), jnp.bfloat16),
            pltpu.VMEM((1, width), jnp.float32),
            pltpu.VMEM((block, width), jnp.bfloat16),
            pltpu.VMEM((n_rep - 1, block, width), jnp.bfloat16),
            pltpu.VMEM((n_rep - 1, block, width), jnp.bfloat16),
            pltpu.VMEM((n_rep,) + whole, jnp.float32),
            pltpu.VMEM((n_rep - 1,) + whole, jnp.float32),
            pltpu.VMEM((steps,) + whole, jnp.float32),
            pltpu.VMEM((steps,) + whole, jnp.float32),
            pltpu.VMEM((2, 1, width), jnp.float32),
            pltpu.VMEM((n_rep + n_rows - 2, 1, width), jnp.float32),
            pltpu.VMEM((2, pairs, 16, 128), jnp.float32),
            pltpu.VMEM((pairs, 16, 128), jnp.float32),
            pltpu.VMEM((pairs, 16, 128), jnp.bfloat16),
            pltpu.VMEM((pairs - 1, 16, 128), jnp.bfloat16),
            pltpu.VMEM((2, pairs, 16, 128), jnp.bfloat16),
            pltpu.SMEM(tile_row.shape, jnp.int32),
            pltpu.SMEM(tile_col.shape, jnp.int32),
            pltpu.SMEM(tile_count.shape, jnp.int32),
            dma((8,)),
            dma((n_rows,)), dma((n_rows,)),
            dma((n_rep - 1,)), dma((n_rep - 1,)),
            dma((n_rep - 1,)), dma((n_rep - 1,)),
            dma((steps,)), dma((steps,)),
            dma((n_rep - 1,)), dma((n_rep - 1,)),
            dma((8,)),
            dma((2, n_rep + n_rows - 2)),
        ],
        compiler_params=pltpu.CompilerParams(
            collective_id=0, has_side_effects=True, vmem_limit_bytes=62 * 1024 * 1024),
    )(features, weight, bias_terms.reshape(1, width), tile_data, tile_row, tile_col, tile_count, grad_out)
    layer_out, weight_grad, bias_grad = pl.pallas_call(
        deliver,
        out_shape=tuple(jax.ShapeDtypeStruct(x.shape, x.dtype) for x in (layer_out, weight_grad, bias_grad)),
        in_specs=[vmem] * 3,
        out_specs=(vmem,) * 3,
    )(layer_out, weight_grad, bias_grad)
    return layer_out, weight_grad, bias_grad.reshape(width)


def solution(mesh):
    placed = (
        P(("rows", "rep"), None),
        P(),
        P(),
        P("rows", None, None, None, None),
        P("rows", None, None),
        P("rows", None, None),
        P("rows", None),
        P(("rows", "rep"), None),
    )
    return jax.shard_map(
        shards,
        mesh=mesh,
        in_specs=placed,
        out_specs=(P(("rows", "rep"), None), P(), P()),
        check_vma=False,
    )
```
